256 devices in a mesh: sect: 4 (over y), grp: 8 (over x, core), tp: 8 (over z).
Axes of the slice: x: 4, y: 4, z: 8, core: 2. Of those that a mesh axis runs over, the one named last changes fastest.
Arguments:
- prefix_tokens: bfloat16 [128, 256, 8192], P(('sect', 'grp'), None, 'tp'), may hold values from -8 to 8
- prefix_lengths: int32 [32], replicated, may hold values from 1 to 256, 5120 in all
- assignment: int32 [32, 1], replicated, may hold values from 0 to 23; in each aligned block of 32 rows (0 to 31, 32 to 63, ...) at most 3 rows name the same one
- norm_gain: bfloat16 [8192], P('tp'), may hold values from 0.099609375 to 1.8984375
- kv_weight: bfloat16 [8192, 2048], P('tp'), as said below
- query_weight: bfloat16 [8192, 8192], P(('sect', 'grp'), 'tp'), as said below
- decode_tokens: bfloat16 [32, 3, 8, 2, 8192], P(('sect', 'grp'), None, None, None, 'tp'), may hold values from -8 to 8
Outputs:
- completion_states: bfloat16 [32, 3, 8, 2, 8192], P(('sect', 'grp'), None, None, None, 'tp')
The draws below stay inside these ranges and needn't reach their ends.
Inputs may be any that keep to these rules, and one draw needn't show every extreme that they name: `assignment`: each decode group takes at most 3 prefixes, and some group takes exactly 3. `prefix_lengths`: the longest prefix has exactly 256 tokens. `query_weight`: entries are at most 4 / sqrt(8192) in magnitude. `kv_weight`: entries are at most 4 / sqrt(8192) in magnitude.
All inputs are finite; a program needn't handle non-finite values.
Results may differ from the reference program's by a relative error of at most 0.0066.
Values may be sent and summed in bfloat16 or wider, within the bound.
A program may use at most 128 MiB of HBM per device.

```python
import math
import jax
import jax.numpy as jnp
import numpy as np
from jax import lax

D = 8192
H = 64
KVH = 8
HD = 128
PP = 4
L = 256
SLOTS = 3
COMP = 8
STEPS = 2
PREFIXES = 32
DGROUPS = 24
ALLGROUPS = 32
N_SECT = 4
N_GRP = 8


def feature_ramp(low, high):
    ramp = jnp.arange(D, dtype=jnp.float32) / (D - 1)
    return low * jnp.exp(ramp * jnp.log(high / low))


def draw_prefix_tokens(key, part):
    key = jax.random.fold_in(key, 21)
    normal_key = jax.random.fold_in(key, 0)
    extent = (ALLGROUPS * PP, L, D)
    entries = jax.random.normal(normal_key, extent, jnp.float32)
    entries = entries * feature_ramp(0.5, 2.0)
    return jnp.clip(entries, -8.0, 8.0).astype(jnp.bfloat16)


def draw_decode_tokens(key, part):
    key = jax.random.fold_in(key, 22)
    normal_key = jax.random.fold_in(key, 0)
    extent = (ALLGROUPS, SLOTS, COMP, STEPS, D)
    entries = jax.random.normal(normal_key, extent, jnp.float32)
    return jnp.clip(entries, -8.0, 8.0).astype(jnp.bfloat16)


def draw_query_weight(key, part):
    key = jax.random.fold_in(key, 23)
    normal_key = jax.random.fold_in(key, 0)
    entries = jnp.clip(jax.random.normal(normal_key, (D, H * HD), jnp.float32), -4.0, 4.0) * (1.0 / D ** 0.5)
    return entries.astype(jnp.bfloat16)


def draw_kv_weight(key, part):
    key = jax.random.fold_in(key, 24)
    normal_key = jax.random.fold_in(key, 0)
    entries = jnp.clip(jax.random.normal(normal_key, (D, 2 * KVH * HD), jnp.float32), -4.0, 4.0) * (1.0 / D ** 0.5)
    return entries.astype(jnp.bfloat16)


def profile(amount, total, most, slope):
    loads = [(1 << 20) // math.isqrt(rank ** slope) + 1 for rank in range(2, amount + 1)]
    spare, counts = total - most - (amount - 1), [1] * (amount - 1)
    while spare > 0:
        free = [i for i in range(amount - 1) if counts[i] < most]
        whole, left = sum([loads[i] for i in free]), spare
        for i in free:
            extra = min(most - counts[i], max(1, left * loads[i] // whole), spare)
            counts[i] = counts[i] + extra
            spare = spare - extra
    return np.array([most] + counts)


def uneven_parts(rng, number_of, total, reach, lean):
    if number_of == 2:
        one = jax.random.randint(rng, (), max(1, total - reach), min(reach, total - 1) + 1)
        return jnp.stack([one, total - one])
    tallies = jnp.asarray(profile(number_of, total, reach, lean), jnp.int32)
    couples = (number_of - 1) // 2
    source_of, receiver = tallies[1:1 + 2 * couples:2], tallies[2:2 + 2 * couples:2]
    room = jnp.minimum(source_of - 1, reach - receiver)
    passed = jax.random.randint(jax.random.fold_in(rng, 1), (couples,), 0, 1 << 20) % (room + 1)
    tallies = tallies.at[1:1 + 2 * couples:2].set(source_of - passed).at[2:2 + 2 * couples:2].set(receiver + passed)
    return tallies[jax.random.permutation(jax.random.fold_in(rng, 2), number_of)]


def shared_out(own_key, own, number, rows, number_of, top, bound, skew):
    ranking = jax.random.permutation(own_key, number_of)
    packed, common = load_shares(number_of, rows * top, bound, skew, True), load_shares(number_of, rows * top, bound, skew, False)
    places = jnp.arange(number_of)

    def named(sizes, turn):
        used = int((sizes > 0).sum())
        fixed = max(1, used // 4)
        shifted = fixed + (places - fixed + turn * (used - fixed)) % max(1, number_of - fixed)
        return jnp.zeros((number_of,), jnp.int32).at[ranking[jnp.where(places < fixed, places, shifted)]].set(jnp.asarray(sizes, jnp.int32))

    sizes = jnp.where(number % 4 == 0, named(packed, number // 4), named(common, number - number // 4 - 1))
    mixed = jax.random.permutation(jax.random.fold_in(own, 3), number_of)
    donor, taker = mixed[0:number_of // 2 * 2:2], mixed[1:number_of // 2 * 2:2]
    room = jnp.minimum(sizes[donor] - 1, bound - sizes[taker]) // 2
    room = jnp.where((donor == ranking[0]) | (taker == ranking[0]) | (sizes[taker] == 0), 0, jnp.maximum(room, 0))
    shifted = jax.random.randint(jax.random.fold_in(own, 4), (number_of // 2,), 0, 1 << 20) % (room + 1)
    sizes = sizes.at[donor].add(-shifted).at[taker].add(shifted)
    members = jnp.searchsorted(jnp.cumsum(sizes), jnp.arange(rows * top), side="right").astype(jnp.int32)
    listing = members.reshape(top, rows).T
    listing = listing[jax.random.permutation(jax.random.fold_in(own, 1), rows)]
    turn = jax.random.randint(jax.random.fold_in(own, 2), (rows, 1), 0, top)
    return jnp.take_along_axis(listing, (jnp.arange(top)[None, :] + turn) % top, axis=1)


def load_shares(number_of, total, limit, slope, full):
    loads = [(1 << 20) // math.isqrt(rank ** slope) + 1 for rank in range(1, number_of + 1)]
    largest = limit if full else min(limit, max(-(-total // number_of), total * loads[0] // sum(loads)))
    least = 1 if total - largest >= number_of - 1 else 0
    holding, rest = [largest] + [least] * (number_of - 1), total - largest - least * (number_of - 1)
    while rest > 0:
        movable = [i for i in range(1, number_of) if holding[i] < largest] or [i for i in range(1, number_of) if holding[i] < limit]
        mass, budget = sum([loads[i] for i in movable]), rest
        for i in movable:
            addition = min(limit - holding[i], max(1, budget * loads[i] // mass), rest)
            holding[i] = holding[i] + addition
            rest = rest - addition
    return np.array(holding)


def setup_inputs(seed: int = 0) -> dict:
    streams_of = jax.random.split(jax.random.key(seed), 8)
    prefix_tokens = draw_prefix_tokens(jax.random.fold_in(streams_of[7], 71), 0)
    prefix_lengths = uneven_parts(streams_of[1], PREFIXES, PREFIXES * L * 5 // 8, L, 2).astype(jnp.int32)
    assignment_keys = jax.random.split(jax.random.fold_in(streams_of[2], 1), PREFIXES // PREFIXES)
    assignment_turns = jax.random.permutation(jax.random.fold_in(streams_of[2], 3), PREFIXES // PREFIXES)
    assignment = jax.vmap(lambda own, number: shared_out(jax.random.fold_in(streams_of[2], 2), own, number, PREFIXES, DGROUPS, 1, SLOTS, 2))(assignment_keys, assignment_turns).reshape((PREFIXES, 1))
    norm_gain = jnp.clip(1.0 + 0.18 * jax.random.normal(streams_of[3], (D,), jnp.float32), 0.099609375, 1.8984375).astype(jnp.bfloat16)
    kv_weight = draw_kv_weight(jax.random.fold_in(streams_of[7], 71), 0)
    query_weight = draw_query_weight(jax.random.fold_in(streams_of[7], 71), 0)
    decode_tokens = draw_decode_tokens(jax.random.fold_in(streams_of[7], 71), 0)
    return dict(prefix_tokens=prefix_tokens, prefix_lengths=prefix_lengths, assignment=assignment, norm_gain=norm_gain, kv_weight=kv_weight, query_weight=query_weight, decode_tokens=decode_tokens)


def rms_rows(rows, gain):
    values = rows.astype(jnp.float32)
    scale = lax.rsqrt(lax.optimization_barrier(jnp.mean(values * values, axis=-1, keepdims=True)) + 1e-05)
    return (values * scale * gain.astype(jnp.float32)).astype(jnp.bfloat16)

def slot_select(assign, group, slots):
    owned = (assign == group).astype(jnp.int32)
    count = owned.shape[0]
    order = jnp.arange(count, dtype=jnp.int32)
    before = (order[None, :] < order[:, None]).astype(jnp.int32)
    rank = lax.optimization_barrier(jnp.sum(before * owned[None, :], axis=1))
    place = jnp.arange(slots, dtype=jnp.int32)
    return ((owned[None, :] == 1) & (rank[None, :] == place[:, None])).astype(jnp.float32)

def attend(query, keyt, valt, own_k, own_v, slot_len):
    inv = 1.0 / query.shape[-1] ** 0.5
    q32 = query.astype(jnp.float32)
    pre = jnp.einsum('jcsagd,jadl->jcsagl', q32, keyt.astype(jnp.float32)) * inv
    own = jnp.einsum('jcsagd,jctad->jcsagt', q32, own_k.astype(jnp.float32)) * inv
    length = keyt.shape[-1]
    steps = own.shape[-1]
    pos = jnp.arange(length, dtype=jnp.float32)
    mask_pre = (pos[None, :] < slot_len[:, None])[:, None, None, None, None, :]
    tri = jnp.arange(steps)[:, None] >= jnp.arange(steps)[None, :]
    mask_own = tri[None, None, :, None, None, :]
    top = jnp.maximum(lax.optimization_barrier(jnp.max(jnp.where(mask_pre, pre, -jnp.inf), axis=-1)), lax.optimization_barrier(jnp.max(jnp.where(mask_own, own, -jnp.inf), axis=-1)))[..., None]
    e_pre = jnp.where(mask_pre, jnp.exp(pre - top), 0.0)
    e_own = jnp.where(mask_own, jnp.exp(own - top), 0.0)
    total = lax.optimization_barrier(jnp.sum(e_pre, axis=-1, keepdims=True)) + lax.optimization_barrier(jnp.sum(e_own, axis=-1, keepdims=True))
    w_pre = (e_pre / total).astype(jnp.bfloat16).astype(jnp.float32)
    w_own = (e_own / total).astype(jnp.bfloat16).astype(jnp.float32)
    out = jnp.einsum('jcsagl,jadl->jcsagd', w_pre, valt.astype(jnp.float32))
    out = out + jnp.einsum('jcsagt,jctad->jcsagd', w_own, own_v.astype(jnp.float32))
    return out.astype(jnp.bfloat16)

def reference(prefix_tokens, prefix_lengths, assignment, norm_gain, kv_weight, query_weight, decode_tokens):
    count = PP * N_GRP
    groups = (N_SECT - 1) * N_GRP
    length = prefix_tokens.shape[1]
    width = prefix_tokens.shape[2]
    heads_kv = kv_weight.shape[1] // (2 * HD)
    per_group = H // heads_kv
    normed = rms_rows(prefix_tokens[:count].reshape(count * length, width), norm_gain)
    prefix_kv = jnp.dot(normed, kv_weight, preferred_element_type=jnp.float32).astype(jnp.bfloat16)
    prefix_kv = prefix_kv.reshape(count, length, heads_kv, 2, HD)
    slots, comp, steps = (decode_tokens.shape[1], decode_tokens.shape[2], decode_tokens.shape[3])
    dec_rows = decode_tokens[N_GRP:].reshape(groups * slots * comp * steps, width)
    dec_norm = rms_rows(dec_rows, norm_gain)
    query = jnp.dot(dec_norm, query_weight, preferred_element_type=jnp.float32).astype(jnp.bfloat16)
    query = query.reshape(groups, slots, comp, steps, heads_kv, per_group, HD)
    dec_kv = jnp.dot(dec_norm, kv_weight, preferred_element_type=jnp.float32).astype(jnp.bfloat16)
    dec_kv = dec_kv.reshape(groups, slots, comp, steps, heads_kv, 2, HD)
    assign = assignment[:, 0]
    lengths = prefix_lengths.astype(jnp.float32)

    def one_group(index):
        select = slot_select(assign, index, slots)
        cache = jnp.einsum('jp,plaed->jaedl', select, prefix_kv.astype(jnp.float32)).astype(jnp.bfloat16)
        slot_len = jnp.dot(select, lengths, precision=lax.Precision.HIGHEST)
        out = attend(query[index], cache[:, :, 0], cache[:, :, 1], dec_kv[index][..., 0, :], dec_kv[index][..., 1, :], slot_len)
        return out.reshape(slots, comp, steps, H * HD)
    decoded = lax.map(one_group, jnp.arange(groups, dtype=jnp.int32))
    zeros = jnp.zeros((N_GRP, slots, comp, steps, H * HD), jnp.bfloat16)
    return jnp.concatenate([zeros, decoded], axis=0)
```

```python
import functools

import jax
import jax.numpy as jnp
from jax import lax
from jax.experimental import pallas as pl
from jax.experimental.pallas import tpu as pltpu
from jax.sharding import PartitionSpec as P

MESH = pl.DeviceIdType.MESH
F32 = jnp.float32
BF16 = jnp.bfloat16
H, KVH, HD = 64, 8, 128
NT = 8
ROWS = 48
EPS = 1e-05


def kernel(
    assign,
    lens,
    gain,
    dec,
    tok,
    wkv,
    wq,
    out,
    wkv_v,
    tokv,
    xp,
    xag,
    xin,
    wq_v,
    ssp,
    ssd,
    dks,
    dkr,
    qs,
    qr,
    send_l,
    recv_l,
    send_s,
    recv_s,
    kv,
    lsem,
    ssem,
    rsem,
):
    s, g, t = lax.axis_index("sect"), lax.axis_index("grp"), lax.axis_index("tp")
    core = lax.rem(g, 2)
    sib = g + 1 - 2 * core
    xr, xl = lax.rem(g + 2, 8), lax.rem(g + 6, 8)
    xo = lax.rem(g + 4, 8)

    def zed(k):
        return lax.rem(t + (k + 2 * NT), NT)

    def sec(k):
        return lax.rem(s + k, 4)

    counts = {"s": 0, "r": 0}

    def new(kind, number=1):
        first = counts[kind]
        counts[kind] += number
        return first

    pending = []

    def remote(src, dst, snd, rcv, dev):
        return pltpu.make_async_remote_copy(
            src_ref=src,
            dst_ref=dst,
            send_sem=ssem.at[snd],
            recv_sem=rsem.at[rcv],
            device_id=dev,
            device_id_type=MESH,
        )

    def push(src, dst, rcv, dev, like, guard=None):
        snd = new("s")
        remote(src, dst, snd, rcv, dev).start()
        pending.append((guard, like, snd))

    def arrive(dst, rcv):
        remote(dst, dst, 0, rcv, (s, sib, t)).wait_recv()

    def when(cond):
        return pl.when(cond)

    decoding = s > 0
    root = s == 0
    first, third = s == 1, s == 3
    side = first | third

    load_wkv = pltpu.make_async_copy(wkv, wkv_v, lsem.at[0])
    load_wkv.start()
    load_wq = pltpu.make_async_copy(wq, wq_v.at[pl.ds(g * 256, 256)], lsem.at[1])
    load_wq.start()

    def load_tok(i):
        return pltpu.make_async_copy(tok.at[2 * i], tokv.at[i], lsem.at[2 + i])

    @when(root)
    def _():
        load_tok(0).start()
        load_tok(1).start()

    barrier = pltpu.get_barrier_semaphore()
    friends = [(s, g, zed(k)) for k in range(1, NT)]
    friends += [(sec(k), g, t) for k in (1, 2, 3)]
    friends += [(s, xr, t), (s, xl, t), (s, sib, t)]
    for dev in friends:
        pl.semaphore_signal(barrier, inc=1, device_id=dev, device_id_type=MESH)
    pl.semaphore_wait(barrier, len(friends))

    r_tok = new("r", 2)
    HB = 128

    def tok_half():
        return tokv.at[0, 0:HB]

    def w_block():
        return wq_v.at[0:256]

    def w_half():
        return wq_v.at[0:128]

    def kv_half():
        return kv.at[0, 0:128]

    @when(root)
    def _():
        for u in range(2):
            rows = pl.ds(u * HB, HB)
            push(tok.at[1, rows], tokv.at[0, rows], r_tok + u, (1, g, t), tok_half, root)
            push(tok.at[3, rows], tokv.at[0, rows], r_tok + u, (3, g, t), tok_half, root)

    r_w = new("r", 5)
    r_ws = new("r", 4)
    mine = pl.ds(g * 256, 256)
    push(wq, wq_v.at[mine], r_w, (s, xr, t), w_block)
    push(wq, wq_v.at[mine], r_w + 1, (s, xl, t), w_block)
    push(wq, wq_v.at[mine], r_ws, (s, sib, t), w_block)

    gain_f = gain[...].astype(F32)
    ones = jnp.ones((8, 1024), BF16)
    nt_dims = (((1,), (1,)), ((), ()))

    r_xag = new("r", 8)
    r_ssd = new("r", 8)
    r_dkv = new("r", 8)
    r_xin = new("r", 6)

    def to_section(shift):
        q = zed(shift)
        dest = q // 2
        snd = new("s")
        rcv = r_xin + (s - 1) * 2 + lax.rem(q, 2)
        src = xag.at[q]
        dst = xin.at[lax.rem(q, 2), pl.ds((s - 1) * ROWS, ROWS)]

        @when(dest != s)
        def _():
            remote(src, dst, snd, rcv, (dest, g, t)).start()

        pending.append((lambda: decoding & (zed(shift) // 2 != s), lambda: xag.at[0], snd))

    @when(decoding)
    def _():
        x = dec[...].astype(F32)
        xag[t] = (x * gain_f).astype(BF16)
        push(xag.at[t], xag.at[t], r_xag, (s, g, zed(1)), lambda: xag.at[0], decoding)
        push(xag.at[t], xag.at[t], r_xag + 4, (s, g, zed(-1)), lambda: xag.at[0], decoding)
        to_section(0)
        square = lax.dot_general(
            ones, (x * x).astype(BF16), nt_dims, preferred_element_type=F32
        )
        ssd[t] = jnp.concatenate([square, jnp.zeros((8, 128 - ROWS), F32)], axis=1)
        for k in range(1, NT):
            push(ssd.at[t], ssd.at[t], r_ssd + k, (s, g, zed(k)), lambda: ssd.at[0], decoding)

    load_wkv.wait()

    @when(decoding)
    def _():
        for a in range(NT):
            dks[a] = jnp.dot(
                xag[t], wkv_v[:, a * 256 : (a + 1) * 256], preferred_element_type=F32
            ).astype(BF16)
        for k in range(1, NT):
            a = zed(k)
            push(dks.at[a], dkr.at[t], r_dkv + k, (s, g, a), lambda: dks.at[0], decoding)
        for k in range(1, 5):
            low, high = zed(-k), zed(k)
            arrive(xag.at[low], r_xag + k - 1)
            if k < 4:
                push(xag.at[low], xag.at[low], r_xag + k, (s, g, zed(1)), lambda: xag.at[0], decoding)
                arrive(xag.at[high], r_xag + 4 + k - 1)
                if k < 3:
                    push(xag.at[high], xag.at[high], r_xag + 4 + k, (s, g, zed(-1)), lambda: xag.at[0], decoding)
                to_section(k)
            to_section(-k)

    def forward_w():
        left, right = pl.ds(xl * 256, 128), pl.ds(xr * 256 + 128, 128)
        arrive(wq_v.at[pl.ds(xl * 256, 256)], r_w)
        push(wq_v.at[left], wq_v.at[left], r_w + 2, (s, xr, t), w_half)
        arrive(wq_v.at[pl.ds(xr * 256, 256)], r_w + 1)
        push(wq_v.at[right], wq_v.at[right], r_w + 3, (s, xl, t), w_half)
        whole = pl.ds(xl * 256, 256)
        push(wq_v.at[whole], wq_v.at[whole], r_ws + 1, (s, sib, t), w_block)
        whole = pl.ds(xr * 256, 256)
        push(wq_v.at[whole], wq_v.at[whole], r_ws + 2, (s, sib, t), w_block)

    def finish_w():
        load_wq.wait()
        arrive(wq_v.at[pl.ds(xo * 256, 128)], r_w + 2)
        arrive(wq_v.at[pl.ds(xo * 256 + 128, 128)], r_w + 3)
        whole = pl.ds(xo * 256, 256)
        push(wq_v.at[whole], wq_v.at[whole], r_ws + 3, (s, sib, t), w_block)
        for n, other in enumerate((g, xl, xr, xo)):
            block = other + 1 - 2 * core
            arrive(wq_v.at[pl.ds(block * 256, 256)], r_ws + n)

    r_long = new("r", 8)
    r_short = new("r", 6)
    r_ssp = new("r", 16)

    def part(i, head):
        return jnp.dot(
            xp[i],
            wkv_v[:, pl.ds(pl.multiple_of(head * 256, 256), 256)],
            preferred_element_type=F32,
        )

    def prepare(i, guard):
        rows = tokv[i].astype(F32)
        xp[i] = (rows * gain_f).astype(BF16)
        ssp[i, t] = lax.dot_general(
            ones, (rows * rows).astype(BF16), nt_dims, preferred_element_type=F32
        )
        for k in range(1, NT):
            push(ssp.at[i, t], ssp.at[i, t], r_ssp + 8 * i + k, (s, g, zed(k)), lambda: ssp.at[0, 0], guard)

    def ring(i, k, guard):
        way = -1 if i == 0 else 1
        if k < 4:
            value = part(i, zed(way * (4 - k)))
            if k > 0:
                arrive(recv_l.at[i, k - 1], r_long + 4 * i + k - 1)
                value = value + recv_l[i, k - 1].astype(F32)
            send_l[i, k] = value.astype(BF16)
            push(send_l.at[i, k], recv_l.at[i, k], r_long + 4 * i + k, (s, g, zed(way)), lambda: send_l.at[0, 0], guard)
        if k < 3:
            value = part(i, zed(-way * (3 - k)))
            if k > 0:
                arrive(recv_s.at[i, k - 1], r_short + 3 * i + k - 1)
                value = value + recv_s[i, k - 1].astype(F32)
            send_s[i, k] = value.astype(BF16)
            push(send_s.at[i, k], recv_s.at[i, k], r_short + 3 * i + k, (s, g, zed(-way)), lambda: send_l.at[0, 0], guard)

    def column(row):
        return jnp.broadcast_to(row, (128, 128)).T

    def settle(i, slot):
        value = part(i, t)
        total = jnp.zeros((8, 256), F32)
        for k in range(1, NT):
            arrive(ssp.at[i, zed(-k)], r_ssp + 8 * i + k)
        for n in range(NT):
            total = total + ssp[i, n]
        scale = lax.rsqrt(total[0:1] / (NT * 1024) + EPS)
        arrive(recv_l.at[i, 3], r_long + 4 * i + 3)
        arrive(recv_s.at[i, 2], r_short + 3 * i + 2)
        value = value + recv_l[i, 3].astype(F32) + recv_s[i, 2].astype(F32)
        for u in range(2):
            by = column(scale[:, u * 128 : (u + 1) * 128])
            half = value[u * 128 : (u + 1) * 128]
            kv[slot, u * 128 : (u + 1) * 128] = jnp.concatenate(
                [half[:, :128] * by, half[:, 128:] * by], axis=1
            ).astype(BF16)

    r_y = new("r", 4)
    here = [4 * g + j for j in range(4)]

    def send_y(j, sections, guard):
        for dest in sections:
            push(kv.at[here[j]], kv.at[here[j]], r_y + j, (dest, g, t), lambda: kv.at[0], guard)

    r_q = new("r", 4)

    def queries():
        finish_w()

        @when(decoding)
        def _():
            for b in range(2):
                xin[b, pl.ds((s - 1) * ROWS, ROWS)] = xag[2 * s + b]

        for other in (1, 2, 3):

            @when(s != other)
            def _():
                for b in range(2):
                    arrive(
                        xin.at[b, (other - 1) * ROWS : other * ROWS], r_xin + (other - 1) * 2 + b
                    )

        for n in range(4):
            cols = slice(n * 256, (n + 1) * 256)
            value = jnp.dot(xin[0], wq_v[0:1024, cols], preferred_element_type=F32)
            value = value + jnp.dot(xin[1], wq_v[1024:2048, cols], preferred_element_type=F32)
            for dest in range(3):
                qs[dest, :, cols] = value[dest * ROWS : (dest + 1) * ROWS].astype(BF16)
        for dest in (1, 2, 3):
            snd = new("s")

            @when(s != dest)
            def _():
                remote(qs.at[dest - 1], qr.at[s], snd, r_q + s, (dest, g, t)).start()

            pending.append((s != dest, lambda: qs.at[0], snd))

    @when(root)
    def _():
        load_tok(0).wait()
        prepare(0, root)
        ring(0, 0, root)
        ring(0, 1, root)
        load_tok(1).wait()
        prepare(1, root)

    @when(side)
    def _():
        for u in range(2):
            arrive(tokv.at[0, u * HB : (u + 1) * HB], r_tok + u)
        prepare(0, side)
        ring(0, 0, side)
        ring(0, 1, side)

    forward_w()

    @when(root)
    def _():
        ring(0, 2, root)
        ring(1, 0, root)
        ring(0, 3, root)
        ring(1, 1, root)
        settle(0, here[0])
        send_y(0, (1, 3), root)
        ring(1, 2, root)

    @when(side)
    def _():
        ring(0, 2, side)
        ring(0, 3, side)

        @when(s == 1)
        def _():
            settle(0, here[1])
            send_y(1, (2, 3), first)

        @when(s == 3)
        def _():
            settle(0, here[3])
            send_y(3, (2, 1), third)

    queries()

    @when(root)
    def _():
        ring(1, 3, root)
        settle(1, here[2])
        send_y(2, (1, 3), root)

    r_x = new("r", 16)
    r_c = new("r", 16)

    def entry(j):
        if j == 0:

            @when(decoding)
            def _():
                arrive(kv.at[here[0]], r_y)

            @when(s == 1)
            def _():
                send_y(0, (2,), first)
        elif j == 2:

            @when(decoding)
            def _():
                arrive(kv.at[here[2]], r_y + 2)

            @when(s == 3)
            def _():
                send_y(2, (2,), third)
        else:

            @when(decoding & (s != j))
            def _():
                arrive(kv.at[here[j]], r_y + j)

        @when(decoding)
        def _():
            block = kv.at[here[j]]
            push(block, block, r_x + 4 * j, (s, xr, t), lambda: kv.at[0], decoding)
            push(block, block, r_x + 4 * j + 1, (s, xl, t), lambda: kv.at[0], decoding)
            push(block, block, r_c + 4 * j, (s, sib, t), lambda: kv.at[0], decoding)

    def relay(j):
        left, right = 4 * xl + j, 4 * xr + j
        arrive(kv.at[left], r_x + 4 * j)
        part_l = kv.at[left, 0:128]
        push(part_l, part_l, r_x + 4 * j + 2, (s, xr, t), kv_half, decoding)
        arrive(kv.at[right], r_x + 4 * j + 1)
        part_r = kv.at[right, 128:256]
        push(part_r, part_r, r_x + 4 * j + 3, (s, xl, t), kv_half, decoding)
        push(kv.at[left], kv.at[left], r_c + 4 * j + 1, (s, sib, t), lambda: kv.at[0], decoding)
        push(kv.at[right], kv.at[right], r_c + 4 * j + 2, (s, sib, t), lambda: kv.at[0], decoding)

    def opposite(j):
        block = 4 * xo + j
        arrive(kv.at[block, 0:128], r_x + 4 * j + 2)
        arrive(kv.at[block, 128:256], r_x + 4 * j + 3)
        push(kv.at[block], kv.at[block], r_c + 4 * j + 3, (s, sib, t), lambda: kv.at[0], decoding)

    def crossed(j):
        for n, other in enumerate((g, xl, xr, xo)):
            arrive(kv.at[4 * (other + 1 - 2 * core) + j], r_c + 4 * j + n)

    for j in (0, 1, 3):
        entry(j)

    @when(decoding)
    def _():
        relay(0)

    entry(2)

    @when(decoding)
    def _():
        relay(1)
        relay(3)
        opposite(0)
        relay(2)
        opposite(1)
        opposite(3)
        opposite(2)

    inv = 1.0 / HD**0.5

    @when(root)
    def _():
        out[...] = jnp.zeros(out.shape, out.dtype)

    @when(decoding)
    def _():
        for k in range(1, NT):
            arrive(ssd.at[zed(-k)], r_ssd + k)
            arrive(dkr.at[zed(-k)], r_dkv + k)
        total = jnp.zeros((8, 128), F32)
        for n in range(NT):
            total = total + ssd[n]
        scale = column(lax.rsqrt(total[0:1] / (NT * 1024) + EPS))[:ROWS]
        dkr[t] = dks[t]
        own = jnp.zeros((ROWS, 256), F32)
        for n in range(NT):
            own = own + dkr[n].astype(F32)
        own_k = (own[:, :128] * scale).astype(BF16)
        own_v = (own[:, 128:] * scale).astype(BF16)
        for src in range(4):

            @when(s != src)
            def _():
                arrive(qr.at[src], r_q + src)

            if src > 0:

                @when(s == src)
                def _():
                    qr[src] = qs[src - 1]

        for j in range(4):
            crossed(j)
        group = (s - 1) * 8 + g

        def pick(p, carry):
            seen, i0, i1, i2, n0, n1, n2 = carry
            hit = (assign[p] == group).astype(jnp.int32)
            length = lens[p]
            h0 = hit * (seen == 0).astype(jnp.int32)
            h1 = hit * (seen == 1).astype(jnp.int32)
            h2 = hit * (seen == 2).astype(jnp.int32)
            return (
                seen + hit,
                i0 + h0 * p,
                i1 + h1 * p,
                i2 + h2 * p,
                n0 + h0 * length,
                n1 + h1 * length,
                n2 + h2 * length,
            )

        zero = jnp.int32(0)
        picked = lax.fori_loop(0, assign.shape[0], pick, (zero,) * 7)
        low = jnp.float32(-1e30)
        pos = lax.broadcasted_iota(jnp.int32, (128, 256), 1)
        row = lax.rem(lax.broadcasted_iota(jnp.int32, (128, 16), 0), 16)
        col = lax.broadcasted_iota(jnp.int32, (128, 16), 1)
        mask_own = (row // 2 == col // 2) & (col <= row)
        for j in range(3):
            rows = slice(j * 16, (j + 1) * 16)
            block = kv[picked[1 + j]]
            keys, values = block[:, :128], block[:, 128:]
            raw = jnp.zeros((16, 1024), F32)
            for src in range(4):
                raw = raw + qr[src, rows].astype(F32)
            by = scale[rows]
            q = jnp.concatenate(
                [raw[:, h * 128 : (h + 1) * 128] * by for h in range(8)], axis=0
            ).astype(BF16)
            pre = lax.dot_general(q, keys, nt_dims, preferred_element_type=F32) * inv
            self_ = lax.dot_general(q, own_k[rows], nt_dims, preferred_element_type=F32) * inv
            mask_pre = pos < picked[4 + j]
            pre = jnp.where(mask_pre, pre, low)
            self_ = jnp.where(mask_own, self_, low)
            top = jnp.maximum(
                jnp.max(pre, axis=1, keepdims=True), jnp.max(self_, axis=1, keepdims=True)
            )
            e_pre = jnp.where(mask_pre, jnp.exp(pre - top), 0.0)
            e_own = jnp.where(mask_own, jnp.exp(self_ - top), 0.0)
            norm = jnp.sum(e_pre, axis=1, keepdims=True) + jnp.sum(e_own, axis=1, keepdims=True)
            w_pre = (e_pre / norm).astype(BF16)
            w_own = (e_own / norm).astype(BF16)
            o = jnp.dot(w_pre, values, preferred_element_type=F32)
            o = o + jnp.dot(w_own, own_v[rows], preferred_element_type=F32)
            o = o.astype(BF16)
            for h in range(8):
                out[rows, h * 128 : (h + 1) * 128] = o[h * 16 : (h + 1) * 16]

    for guard, like, snd in pending:

        def done(like=like, snd=snd):
            remote(like(), like(), snd, 0, (s, sib, t)).wait_send()

        if guard is None:
            done()
        else:
            when(guard() if callable(guard) else guard)(done)

    assert counts["s"] <= N_SEND and counts["r"] <= N_RECV, counts


N_SEND = 200
N_RECV = 140


def local(
    prefix_tokens, prefix_lengths, assignment, norm_gain, kv_weight, query_weight, decode_tokens
):
    shape = decode_tokens.shape
    dec = decode_tokens.reshape(ROWS, 1024)
    smem = pl.BlockSpec(memory_space=pltpu.SMEM)
    vmem = pl.BlockSpec(memory_space=pltpu.VMEM)
    anywhere = pl.BlockSpec(memory_space=pl.ANY)
    result = pl.pallas_call(
        kernel,
        out_shape=jax.ShapeDtypeStruct((ROWS, 1024), BF16),
        in_specs=[smem, smem, vmem, vmem, anywhere, anywhere, anywhere],
        out_specs=vmem,
        scratch_shapes=[
            pltpu.VMEM((1024, 2048), BF16),
            pltpu.VMEM((2, 256, 1024), BF16),
            pltpu.VMEM((2, 256, 1024), BF16),
            pltpu.VMEM((8, ROWS, 1024), BF16),
            pltpu.VMEM((2, 3 * ROWS, 1024), BF16),
            pltpu.VMEM((2048, 1024), BF16),
            pltpu.VMEM((2, 8, 8, 256), F32),
            pltpu.VMEM((8, 8, 128), F32),
            pltpu.VMEM((8, ROWS, 256), BF16),
            pltpu.VMEM((8, ROWS, 256), BF16),
            pltpu.VMEM((3, ROWS, 1024), BF16),
            pltpu.VMEM((4, ROWS, 1024), BF16),
            pltpu.VMEM((2, 4, 256, 256), BF16),
            pltpu.VMEM((2, 4, 256, 256), BF16),
            pltpu.VMEM((2, 3, 256, 256), BF16),
            pltpu.VMEM((2, 3, 256, 256), BF16),
            pltpu.VMEM((32, 256, 256), BF16),
            pltpu.SemaphoreType.DMA((4,)),
            pltpu.SemaphoreType.DMA((N_SEND,)),
            pltpu.SemaphoreType.DMA((N_RECV,)),
        ],
        compiler_params=pltpu.CompilerParams(
            collective_id=0, has_side_effects=True, vmem_limit_bytes=40 * 2**20
        ),
    )(
        assignment[:, 0],
        prefix_lengths,
        norm_gain.reshape(1, 1024),
        dec,
        prefix_tokens,
        kv_weight,
        query_weight,
    )
    return result.reshape(shape)


def solution(mesh):
    placed = (
        P(("sect", "grp"), None, "tp"),
        P(),
        P(),
        P("tp"),
        P("tp", None),
        P(("sect", "grp"), "tp"),
        P(("sect", "grp"), None, None, None, "tp"),
    )
    return jax.shard_map(
        local,
        mesh=mesh,
        in_specs=placed,
        out_specs=P(("sect", "grp"), None, None, None, "tp"),
        check_vma=False,
    )
```

```python
import jax
import jax.numpy as jnp
from jax import lax
from jax.experimental import pallas as pl
from jax.experimental.pallas import tpu as pltpu
from jax.sharding import PartitionSpec as P

MESH = pl.DeviceIdType.MESH
F32 = jnp.float32
BF16 = jnp.bfloat16
HD = 128
NT = 8
ROWS = 48
HALF = 128
EPS = 1e-05
N_SEND = 260
N_RECV = 180


def kernel(
    assign,
    lens,
    gain,
    dec,
    tok,
    wkv,
    wq,
    out,
    wkv_v,
    tokv,
    tokx,
    xp,
    x2,
    pbuf,
    xag,
    xn,
    xin,
    wq_v,
    ssp,
    gains,
    dks,
    dkr,
    qs,
    qr,
    send_l,
    recv_l,
    send_s,
    recv_s,
    kv,
    lsem,
    ssem,
    rsem,
):
    s, g, t = lax.axis_index("sect"), lax.axis_index("grp"), lax.axis_index("tp")
    core = lax.rem(g, 2)
    sib = g + 1 - 2 * core
    xr, xl, xo = lax.rem(g + 2, 8), lax.rem(g + 6, 8), lax.rem(g + 4, 8)

    def zed(k):
        return lax.rem(t + (k + 2 * NT), NT)

    def sec(k):
        return lax.rem(s + k, 4)

    counts = {"s": 0, "r": 0}

    def new(kind, number=1):
        first = counts[kind]
        counts[kind] += number
        return first

    pending = []

    def remote(src, dst, snd, rcv, dev):
        return pltpu.make_async_remote_copy(
            src_ref=src,
            dst_ref=dst,
            send_sem=ssem.at[snd],
            recv_sem=rsem.at[rcv],
            device_id=dev,
            device_id_type=MESH,
        )

    def push(src, dst, rcv, dev, like, guard=None):
        snd = new("s")
        remote(src, dst, snd, rcv, dev).start()
        pending.append((guard, like, snd))

    def arrive(dst, rcv):
        remote(dst, dst, 0, rcv, (s, sib, t)).wait_recv()

    when = pl.when
    decoding, root = s > 0, s == 0
    first, third = s == 1, s == 3
    side, middle = first | third, s == 2

    def tok_half():
        return tokv.at[0, 0:HALF]

    def w_block():
        return wq_v.at[0:256]

    def w_half():
        return wq_v.at[0:128]

    def kv_half():
        return kv.at[0, 0:HALF]

    def kv_whole():
        return kv.at[0]

    def x_chunk():
        return xag.at[0]

    barrier = pltpu.get_barrier_semaphore()
    friends = [(s, g, zed(k)) for k in range(1, NT)]
    friends += [(sec(k), g, t) for k in (1, 2, 3)]
    friends += [(s, xr, t), (s, xl, t), (s, sib, t)]
    for dev in friends:
        pl.semaphore_signal(barrier, inc=1, device_id=dev, device_id_type=MESH)

    def load_tok(i):
        return pltpu.make_async_copy(tok.at[2 * i], tokv.at[i], lsem.at[2 + i])

    def load_out(i):
        return pltpu.make_async_copy(tok.at[2 * i + 1], tokx.at[i], lsem.at[12 + i])

    load_wq = pltpu.make_async_copy(wq, wq_v.at[pl.ds(g * 256, 256)], lsem.at[1])

    def load_wkv(a):
        return pltpu.make_async_copy(
            wkv.at[:, a * 256 : (a + 1) * 256], wkv_v.at[a], lsem.at[4 + a]
        )

    load_wq.start()

    @when(root)
    def _():
        load_tok(0).start()
        load_out(0).start()
        load_out(1).start()

    for a in range(NT):
        load_wkv(a).start()

    @when(root)
    def _():
        load_tok(1).start()

    gain_v = gain[...].astype(F32)
    gain_f = jnp.concatenate([gain_v[n : n + 1] for n in range(8)], axis=1)
    ones = jnp.ones((8, 1024), BF16)
    nt_dims = (((1,), (1,)), ((), ()))

    def column(row):
        return jnp.broadcast_to(row, (128, 128)).T

    gains[t] = gain_v

    @when(decoding)
    def _():
        xag[t] = dec[...]

    def way_of(i):
        return -1 if i == 0 else 1

    def parts(i, first, last, rows=slice(0, 256)):
        def one(n, carry):
            odd = lax.rem(n, 2)
            shift = way_of(i) * (1 - 2 * odd) * (4 - n // 2 - odd)
            head = lax.rem(t + shift + 2 * NT, NT)
            pbuf[i, n, rows] = jnp.dot(xp[i, rows], wkv_v[head], preferred_element_type=F32)
            return carry

        lax.fori_loop(first, last, one, 0)

    def prepare(i, low=0, high=8):
        def one(n, carry):
            rows = pl.ds(pl.multiple_of(n * 32, 32), 32)
            values = tokv[i, rows].astype(F32)
            xp[i, rows] = (values * gain_f).astype(BF16)
            x2[rows] = (values * values).astype(BF16)
            return carry

        lax.fori_loop(low, high, one, 0)

    @when(root)
    def _():
        load_tok(0).wait()
        for a in range(NT):
            load_wkv(a).wait()
        prepare(0)
        parts(0, 0, 2)

    pl.semaphore_wait(barrier, len(friends))

    r_long = new("r", 16)
    r_short = new("r", 12)
    r_ssp = new("r", 16)
    r_gain = new("r", 8)
    r_tok = new("r", 2)
    r_w = new("r", 4)
    r_ws = new("r", 4)
    r_xag = new("r", 8)
    r_dkv = new("r", 8)
    r_xin = new("r", 6)

    @when(root)
    def _():
        for i in range(2):
            load_out(i).wait()
        for u in range(2):
            rows = pl.ds(u * HALF, HALF)
            push(tokx.at[0, rows], tokv.at[0, rows], r_tok + u, (1, g, t), tok_half, root)
            push(tokx.at[1, rows], tokv.at[0, rows], r_tok + u, (3, g, t), tok_half, root)

    mine = pl.ds(g * 256, 256)
    load_wq.wait()
    push(wq_v.at[mine], wq_v.at[mine], r_w, (s, xr, t), w_block)
    push(wq_v.at[mine], wq_v.at[mine], r_w + 1, (s, xl, t), w_block)
    push(wq_v.at[mine], wq_v.at[mine], r_ws, (s, sib, t), w_block)

    def start_x():
        push(xag.at[t], xag.at[t], r_xag, (s, g, zed(1)), x_chunk, decoding)
        push(xag.at[t], xag.at[t], r_xag + 4, (s, g, zed(-1)), x_chunk, decoding)
        for k in range(1, NT):
            push(
                gains.at[t], gains.at[t], r_gain + k, (s, g, zed(k)), lambda: gains.at[0], decoding
            )

    def gather_x(k):
        low, high = zed(-k), zed(k)
        arrive(xag.at[low], r_xag + k - 1)
        if k < 4:
            push(xag.at[low], xag.at[low], r_xag + k, (s, g, zed(1)), x_chunk, decoding)
            arrive(xag.at[high], r_xag + 4 + k - 1)
            if k < 3:
                push(xag.at[high], xag.at[high], r_xag + 4 + k, (s, g, zed(-1)), x_chunk, decoding)

    def normalise():
        for k in range(1, NT):
            arrive(gains.at[zed(-k)], r_gain + k)

        def add(q, total):
            for n in range(8):
                x = xag[q, :, n * 128 : (n + 1) * 128].astype(F32)
                total = total + x * x
            return total

        total = lax.fori_loop(0, NT, add, jnp.zeros((ROWS, 128), F32))
        mean = jnp.sum(total, axis=1, keepdims=True) / (NT * 1024)
        scale = jnp.broadcast_to(lax.rsqrt(mean + EPS), (ROWS, 128))

        def one(q, carry):
            for n in range(8):
                cols = slice(n * 128, (n + 1) * 128)
                x = xag[q, :, cols].astype(F32) * scale * gains[q, n : n + 1]
                xn[q, :, cols] = x.astype(BF16)
            return carry

        lax.fori_loop(0, NT, one, 0)
        place = pl.ds((s - 1) * ROWS, ROWS)
        for dest in range(4):
            snd = new("s", 2)

            @when(s != dest)
            def _():
                for b in range(2):
                    remote(
                        xn.at[2 * dest + b],
                        xin.at[b, place],
                        snd + b,
                        r_xin + (s - 1) * 2 + b,
                        (dest, g, t),
                    ).start()

            for b in range(2):
                pending.append((lambda dest=dest: decoding & (s != dest), x_chunk, snd + b))
        for b in range(2):
            xin[b, place] = xn[2 * s + b]

    def own_partial():
        def one(n, carry):
            a = lax.rem(t + n, NT)
            dks[a] = jnp.dot(xn[t], wkv_v[a], preferred_element_type=F32)
            return carry

        lax.fori_loop(0, NT, one, 0)

    def send_own():
        for k in range(1, NT):
            a = zed(k)
            push(dks.at[a], dkr.at[t], r_dkv + k, (s, g, a), lambda: dks.at[0], decoding)

    def forward_w(guard):
        left, right = pl.ds(xl * 256, 128), pl.ds(xr * 256 + 128, 128)
        arrive(wq_v.at[pl.ds(xl * 256, 256)], r_w)
        push(wq_v.at[left], wq_v.at[left], r_w + 2, (s, xr, t), w_half, guard)
        arrive(wq_v.at[pl.ds(xr * 256, 256)], r_w + 1)
        push(wq_v.at[right], wq_v.at[right], r_w + 3, (s, xl, t), w_half, guard)
        for n, other in ((1, xl), (2, xr)):
            whole = pl.ds(other * 256, 256)
            push(wq_v.at[whole], wq_v.at[whole], r_ws + n, (s, sib, t), w_block, guard)

    def finish_w(guard):
        arrive(wq_v.at[pl.ds(xo * 256, 128)], r_w + 2)
        arrive(wq_v.at[pl.ds(xo * 256 + 128, 128)], r_w + 3)
        whole = pl.ds(xo * 256, 256)
        push(wq_v.at[whole], wq_v.at[whole], r_ws + 3, (s, sib, t), w_block, guard)
        for n, other in enumerate((g, xl, xr, xo)):
            block = other + 1 - 2 * core
            arrive(wq_v.at[pl.ds(block * 256, 256)], r_ws + n)

    def squares(i, guard):
        ssp[i, t] = lax.dot_general(ones, x2[...], nt_dims, preferred_element_type=F32)
        for k in range(1, NT):
            push(
                ssp.at[i, t],
                ssp.at[i, t],
                r_ssp + 8 * i + k,
                (s, g, zed(k)),
                lambda: ssp.at[0, 0],
                guard,
            )

    def ring(i, k, guard, halves=(0, 1)):
        way = way_of(i)
        for u in halves:
            rows = slice(u * HALF, (u + 1) * HALF)
            for short in (0, 1):
                if short and k == 3:
                    continue
                snd, rcv, base, steps, dev = (
                    (send_s, recv_s, r_short, 3, (s, g, zed(-way)))
                    if short
                    else (send_l, recv_l, r_long, 4, (s, g, zed(way)))
                )
                value = pbuf[i, 2 * k + short, rows]
                if k > 0:
                    arrive(rcv.at[i, k - 1, rows], base + (i * steps + k - 1) * 2 + u)
                    value = value + rcv[i, k - 1, rows].astype(F32)
                snd[i, k, rows] = value.astype(BF16)
                push(
                    snd.at[i, k, rows],
                    rcv.at[i, k, rows],
                    base + (i * steps + k) * 2 + u,
                    dev,
                    kv_half,
                    guard,
                )

    def begin(i, guard):
        prepare(i)
        parts(i, 0, 2)
        ring(i, 0, guard)
        parts(i, 2, 8)
        squares(i, guard)

    def settle(i, slot):
        for k in range(1, NT):
            arrive(ssp.at[i, zed(-k)], r_ssp + 8 * i + k)
        total = ssp[i, 0]
        for n in range(1, NT):
            total = total + ssp[i, n]
        scale = lax.rsqrt(total[0:1] / (NT * 1024) + EPS)
        for u in range(2):
            rows = slice(u * HALF, (u + 1) * HALF)
            by = column(scale[:, rows])
            arrive(recv_l.at[i, 3, rows], r_long + (i * 4 + 3) * 2 + u)
            arrive(recv_s.at[i, 2, rows], r_short + (i * 3 + 2) * 2 + u)
            value = pbuf[i, 7, rows] + recv_l[i, 3, rows].astype(F32)
            value = value + recv_s[i, 2, rows].astype(F32)
            kv[slot, rows] = jnp.concatenate(
                [value[:, :128] * by, value[:, 128:] * by], axis=1
            ).astype(BF16)

    r_y = new("r", 4)

    def here(j):
        return 4 * g + j

    def send_y(j, sections, guard):
        for dest in sections:
            push(kv.at[here(j)], kv.at[here(j)], r_y + j, (dest, g, t), kv_whole, guard)

    r_q = new("r", 4)

    def queries(guard):
        finish_w(guard)

        for other in (1, 2, 3):

            @when(s != other)
            def _():
                for b in range(2):
                    arrive(
                        xin.at[b, (other - 1) * ROWS : other * ROWS], r_xin + (other - 1) * 2 + b
                    )

        def one(n, carry):
            cols = pl.ds(pl.multiple_of(n * 256, 256), 256)
            value = jnp.dot(xin[0], wq_v[0:1024, cols], preferred_element_type=F32)
            value = value + jnp.dot(xin[1], wq_v[1024:2048, cols], preferred_element_type=F32)
            for dest in range(3):
                qs[dest, :, cols] = value[dest * ROWS : (dest + 1) * ROWS].astype(BF16)
            return carry

        lax.fori_loop(0, 4, one, 0)

    def answer(guard):
        for dest in (1, 2, 3):
            snd = new("s")

            @when(s != dest)
            def _():
                remote(qs.at[dest - 1], qr.at[s], snd, r_q + s, (dest, g, t)).start()

            pending.append((lambda dest=dest: guard & (s != dest), lambda: qs.at[0], snd))

    @when(decoding)
    def _():
        start_x()
        for a in range(NT):
            load_wkv(a).wait()

    r_x = new("r", 24)
    r_c = new("r", 16)

    near = 1 + 2 * (s // 3)
    far = 4 - near

    def entry(j):
        if isinstance(j, int):
            arrive(kv.at[here(j)], r_y + j)
        else:

            @when(s != j)
            def _():
                arrive(kv.at[here(j)], r_y + j)

        block = kv.at[here(j)]
        top, bottom = kv.at[here(j), 0:HALF], kv.at[here(j), HALF : 2 * HALF]
        push(top, top, r_x + 6 * j, (s, xr, t), kv_half, decoding)
        push(bottom, bottom, r_x + 6 * j + 1, (s, xl, t), kv_half, decoding)
        push(bottom, bottom, r_x + 6 * j + 4, (s, xr, t), kv_half, decoding)
        push(top, top, r_x + 6 * j + 5, (s, xl, t), kv_half, decoding)
        push(block, block, r_c + 4 * j, (s, sib, t), kv_whole, decoding)

    def relay(j):
        left, right = 4 * xl + j, 4 * xr + j
        part_l = kv.at[left, 0:HALF]
        arrive(part_l, r_x + 6 * j)
        push(part_l, part_l, r_x + 6 * j + 2, (s, xr, t), kv_half, decoding)
        part_r = kv.at[right, HALF : 2 * HALF]
        arrive(part_r, r_x + 6 * j + 1)
        push(part_r, part_r, r_x + 6 * j + 3, (s, xl, t), kv_half, decoding)
        arrive(kv.at[left, HALF : 2 * HALF], r_x + 6 * j + 4)
        push(kv.at[left], kv.at[left], r_c + 4 * j + 1, (s, sib, t), kv_whole, decoding)
        arrive(kv.at[right, 0:HALF], r_x + 6 * j + 5)
        push(kv.at[right], kv.at[right], r_c + 4 * j + 2, (s, sib, t), kv_whole, decoding)

    def opposite(j):
        block = 4 * xo + j
        arrive(kv.at[block, 0:128], r_x + 6 * j + 2)
        arrive(kv.at[block, 128:256], r_x + 6 * j + 3)
        push(kv.at[block], kv.at[block], r_c + 4 * j + 3, (s, sib, t), kv_whole, decoding)

    def crossed(j):
        for n, other in enumerate((g, xl, xr, xo)):
            arrive(kv.at[4 * (other + 1 - 2 * core) + j], r_c + 4 * j + n)

    def tokens(u):
        rows = slice(u * HALF, (u + 1) * HALF)
        arrive(tokv.at[0, rows], r_tok + u)
        prepare(0, 4 * u, 4 * u + 4)
        parts(0, 0, 2, rows)
        ring(0, 0, side, (u,))
        parts(0, 2, 8, rows)

    def settle_side():
        settle(0, here(s))

        @when(s == 1)
        def _():
            send_y(1, (2, 3), first)

        @when(s == 3)
        def _():
            send_y(3, (2, 1), third)

    @when(root)
    def _():
        ring(0, 0, root)
        squares(0, root)
        parts(0, 2, 8)
        load_tok(1).wait()
        ring(0, 1, root)
        prepare(1)
        parts(1, 0, 2)
        ring(1, 0, root)
        parts(1, 2, 8)
        ring(0, 2, root)
        ring(1, 1, root)
        squares(1, root)
        ring(0, 3, root)
        ring(1, 2, root)
        forward_w(root)
        settle(0, here(0))
        send_y(0, (1, 3, 2), root)
        ring(1, 3, root)
        settle(1, here(2))
        send_y(2, (1, 3, 2), root)
        queries(root)
        answer(root)

    @when(decoding)
    def _():
        gather_x(1)
        gather_x(2)

        @when(side)
        def _():
            tokens(0)

        gather_x(3)

        @when(side)
        def _():
            ring(0, 1, side, (0,))
            tokens(1)
            squares(0, side)

        forward_w(decoding)
        gather_x(4)
        normalise()

        @when(side)
        def _():
            ring(0, 2, side, (0,))
            ring(0, 1, side, (1,))


        @when(side)
        def _():
            ring(0, 3, side, (0,))
            ring(0, 2, side, (1,))

        own_partial()

        @when(side)
        def _():
            ring(0, 3, side, (1,))

        @when(s == 2)
        def _():
            queries(middle)
            answer(middle)

        entry(0)

        @when(side)
        def _():
            settle_side()

        entry(near)

        @when(side)
        def _():
            queries(side)
            answer(side)

        send_own()

    inv = 1.0 / HD**0.5

    @when(root)
    def _():
        out[...] = jnp.zeros(out.shape, out.dtype)

    @when(decoding)
    def _():
        relay(0)
        entry(2)
        entry(far)
        relay(near)
        opposite(0)
        relay(2)
        relay(far)
        opposite(near)
        opposite(2)
        opposite(far)

        for k in range(1, NT):
            arrive(dkr.at[zed(-k)], r_dkv + k)
        own = dks[t]
        for k in range(1, NT):
            own = own + dkr[zed(k)]
        own_k, own_v = own[:, :128].astype(BF16), own[:, 128:].astype(BF16)
        for src in range(4):

            @when(s != src)
            def _():
                arrive(qr.at[src], r_q + src)

            if src > 0:

                @when(s == src)
                def _():
                    qr[src] = qs[src - 1]

        group = (s - 1) * 8 + g

        def pick(p, carry):
            seen, i0, i1, i2, n0, n1, n2 = carry
            hit = (assign[p] == group).astype(jnp.int32)
            length = lens[p]
            h0 = hit * (seen == 0).astype(jnp.int32)
            h1 = hit * (seen == 1).astype(jnp.int32)
            h2 = hit * (seen == 2).astype(jnp.int32)
            return (
                seen + hit,
                i0 + h0 * p,
                i1 + h1 * p,
                i2 + h2 * p,
                n0 + h0 * length,
                n1 + h1 * length,
                n2 + h2 * length,
            )

        zero = jnp.int32(0)
        picked = lax.fori_loop(0, assign.shape[0], pick, (zero,) * 7)
        low = jnp.float32(-1e30)
        pos = lax.broadcasted_iota(jnp.int32, (128, 256), 1)
        row = lax.rem(lax.broadcasted_iota(jnp.int32, (128, 16), 0), 16)
        col = lax.broadcasted_iota(jnp.int32, (128, 16), 1)
        mask_own = (row // 2 == col // 2) & (col <= row)
        asked, selves = [], []
        for j in range(3):
            rows = slice(j * 16, (j + 1) * 16)
            raw = qr[0, rows].astype(F32)
            for src in range(1, 4):
                raw = raw + qr[src, rows].astype(F32)
            q = jnp.concatenate(
                [raw[:, h * 128 : (h + 1) * 128] for h in range(8)], axis=0
            ).astype(BF16)
            asked.append(q)
            selves.append(
                lax.dot_general(q, own_k[rows], nt_dims, preferred_element_type=F32) * inv
            )
        for j in range(4):
            crossed(j)
        for j in range(3):
            rows = slice(j * 16, (j + 1) * 16)
            block = kv[picked[1 + j]]
            keys, values = block[:, :128], block[:, 128:]
            q, self_ = asked[j], selves[j]
            pre = lax.dot_general(q, keys, nt_dims, preferred_element_type=F32) * inv
            mask_pre = pos < picked[4 + j]
            pre = jnp.where(mask_pre, pre, low)
            self_ = jnp.where(mask_own, self_, low)
            top = jnp.maximum(
                jnp.max(pre, axis=1, keepdims=True), jnp.max(self_, axis=1, keepdims=True)
            )
            e_pre = jnp.where(mask_pre, jnp.exp(pre - top), 0.0)
            e_own = jnp.where(mask_own, jnp.exp(self_ - top), 0.0)
            norm = jnp.sum(e_pre, axis=1, keepdims=True) + jnp.sum(e_own, axis=1, keepdims=True)
            w_pre = (e_pre / norm).astype(BF16)
            w_own = (e_own / norm).astype(BF16)
            o = jnp.dot(w_pre, values, preferred_element_type=F32)
            o = o + jnp.dot(w_own, own_v[rows], preferred_element_type=F32)
            o = o.astype(BF16)
            for h in range(8):
                out[rows, h * 128 : (h + 1) * 128] = o[h * 16 : (h + 1) * 16]

    for guard, like, snd in pending:

        def done(like=like, snd=snd):
            remote(like(), like(), snd, 0, (s, sib, t)).wait_send()

        if guard is None:
            done()
        else:
            when(guard() if callable(guard) else guard)(done)

    assert counts["s"] <= N_SEND and counts["r"] <= N_RECV, counts


def local(
    prefix_tokens, prefix_lengths, assignment, norm_gain, kv_weight, query_weight, decode_tokens
):
    shape = decode_tokens.shape
    smem = pl.BlockSpec(memory_space=pltpu.SMEM)
    vmem = pl.BlockSpec(memory_space=pltpu.VMEM)
    anywhere = pl.BlockSpec(memory_space=pl.ANY)
    result = pl.pallas_call(
        kernel,
        out_shape=jax.ShapeDtypeStruct((ROWS, 1024), BF16),
        in_specs=[smem, smem, vmem, vmem, anywhere, anywhere, anywhere],
        out_specs=vmem,
        scratch_shapes=[
            pltpu.VMEM((8, 1024, 256), BF16),
            pltpu.VMEM((2, 256, 1024), BF16),
            pltpu.VMEM((2, 256, 1024), BF16),
            pltpu.VMEM((2, 256, 1024), BF16),
            pltpu.VMEM((256, 1024), BF16),
            pltpu.VMEM((2, 8, 256, 256), F32),
            pltpu.VMEM((8, ROWS, 1024), BF16),
            pltpu.VMEM((8, ROWS, 1024), BF16),
            pltpu.VMEM((2, 3 * ROWS, 1024), BF16),
            pltpu.VMEM((2048, 1024), BF16),
            pltpu.VMEM((2, 8, 8, 256), F32),
            pltpu.VMEM((8, 8, 128), F32),
            pltpu.VMEM((8, ROWS, 256), F32),
            pltpu.VMEM((8, ROWS, 256), F32),
            pltpu.VMEM((3, ROWS, 1024), BF16),
            pltpu.VMEM((4, ROWS, 1024), BF16),
            pltpu.VMEM((2, 4, 256, 256), BF16),
            pltpu.VMEM((2, 4, 256, 256), BF16),
            pltpu.VMEM((2, 3, 256, 256), BF16),
            pltpu.VMEM((2, 3, 256, 256), BF16),
            pltpu.VMEM((32, 256, 256), BF16),
            pltpu.SemaphoreType.DMA((14,)),
            pltpu.SemaphoreType.DMA((N_SEND,)),
            pltpu.SemaphoreType.DMA((N_RECV,)),
        ],
        compiler_params=pltpu.CompilerParams(
            collective_id=0, has_side_effects=True, vmem_limit_bytes=60 * 2**20
        ),
    )(
        assignment[:, 0],
        prefix_lengths,
        norm_gain.reshape(8, 128),
        decode_tokens.reshape(ROWS, 1024),
        prefix_tokens,
        kv_weight,
        query_weight,
    )
    return result.reshape(shape)


def solution(mesh):
    placed = (
        P(("sect", "grp"), None, "tp"),
        P(),
        P(),
        P("tp"),
        P("tp", None),
        P(("sect", "grp"), "tp"),
        P(("sect", "grp"), None, None, None, "tp"),
    )
    return jax.shard_map(
        local,
        mesh=mesh,
        in_specs=placed,
        out_specs=P(("sect", "grp"), None, None, None, "tp"),
        check_vma=False,
    )
```
